256 devices in a mesh: dp: 4 (over x_lo, core), mp: 64 (over y, z, x_hi).
Axes of the slice: x: 4 (x_hi: 2, x_lo: 2; x = x_hi * 2 + x_lo), y: 4, z: 8, core: 2. Of those that a mesh axis runs over, the one named last changes fastest.
Arguments:
- tokens: bfloat16 [65536, 4608], P('mp', 'dp'), may hold values from -6 to 6
- kv_weight: bfloat16 [2, 4608, 1024], P(None, 'dp', 'mp'), may hold values from -0.25 to 0.25
- d_kv: bfloat16 [65536, 2, 1024], P('mp', None, 'dp'), may hold values from -16 to 16
Outputs:
- kv_out: bfloat16 [65536, 2, 1024], P('mp', None, 'dp')
- d_tokens: bfloat16 [65536, 4608], P('mp', 'dp')
- grad_kv: float32 [2, 4608, 1024], P(None, 'dp', 'mp')
The draws below stay inside these ranges and needn't reach their ends.
All inputs are finite; a program needn't handle non-finite values.
Results may differ from the reference program's by a relative error of at most 0.001.
Values may be sent and summed in bfloat16 or wider, within the bound.
No kernel may reach another device: no remote copies, remote signals or barrier semaphores. Data moves between devices by JAX's collectives and lax.ppermute only.
A program may use at most 128 MiB of HBM per device.

```python
import jax
import jax.numpy as jnp

D = 4608
KVW = 1024
TOKENS = 65536


def raised(array, rng, source, target, shards_of, factor):
    owner, partner = [(jnp.arange(array.shape[position]) // (array.shape[position] // shards_of)).reshape([-1 if axis == position else 1 for axis in range(array.ndim)]) for position in (source, target)]
    chosen = jax.random.permutation(rng, shards_of)[partner]
    strong = (owner == chosen) | (owner == (partner + shards_of // 2) % shards_of)
    return jnp.where(strong, factor * array, array)


def steps_of(key, dims, split, smallest, largest):
    def one(position, parts):
        draws = jax.random.uniform(jax.random.fold_in(jax.random.fold_in(key, 6), position), (parts,), jnp.float32, smallest / len(split), largest / len(split))
        return jnp.repeat(jnp.exp(draws), dims[position] // parts).reshape((-1,) + (1,) * (len(dims) - position - 1))

    level = one(*split[0])
    for cut in split[1:]:
        level = level * one(*cut)
    return level


def noise(own_key, shape, scale, most, split=(), dtype=jnp.bfloat16):
    result = jax.random.normal(own_key, shape, jnp.float32) * scale
    if len(split) > 0:
        result = steps_of(own_key, shape, split, -0.22, 0.18) * result
    return jnp.clip(result, min=-most, max=most).astype(dtype)


def noise_with(key, dims, deviation, limit, pieces, heavy, held_as=jnp.bfloat16):
    values = deviation * jax.random.normal(key, dims, jnp.float32)
    if pieces:
        values = values * steps_of(key, dims, pieces, -0.22, 0.18)
    return jnp.clip(raised(values, jax.random.fold_in(key, 3), *heavy), -limit, limit).astype(held_as)


def setup_inputs(seed: int = 0) -> dict:
    seeds = jax.random.split(jax.random.key(seed), 4)
    tokens = noise(seeds[0], (TOKENS, D), 1.0, 6.0, ((0, 64), (1, 4)))
    kv_weight = noise_with(seeds[1], (2, D, KVW), D ** -0.5, 0.25, ((1, 4), (2, 64)), (1, 2, 64, 4.0))
    d_kv = noise_with(seeds[2], (TOKENS, 2, KVW), 1.0, 16.0, ((0, 64), (2, 4)), (0, 2, 64, 4.0))
    return dict(tokens=tokens, kv_weight=kv_weight, d_kv=d_kv)


def reference(tokens, kv_weight, d_kv):
    joined = jnp.transpose(kv_weight, (1, 0, 2)).reshape(D, 2 * KVW)
    kv_flat = jnp.dot(tokens, joined, preferred_element_type=jnp.float32)
    kv_out = kv_flat.astype(jnp.bfloat16).reshape(TOKENS, 2, KVW)
    d_flat = d_kv.reshape(TOKENS, 2 * KVW)
    d_tokens = jnp.dot(d_flat, joined.T, preferred_element_type=jnp.float32).astype(jnp.bfloat16)
    grad_flat = jnp.dot(tokens.T, d_flat, preferred_element_type=jnp.float32)
    grad_kv = jnp.transpose(grad_flat.reshape(D, 2, KVW), (1, 0, 2))
    return kv_out, d_tokens, grad_kv
```

```python
import jax
import jax.numpy as jnp
from jax import lax
from jax.sharding import Mesh, PartitionSpec as P

MP = ("y", "z", "xh")
DP = ("xl", "core")


def per_device(tokens, kv_weight, d_kv):
    panels = kv_weight
    for axis in ("xh", "z", "y"):
        panels = lax.all_gather(panels, axis, axis=2, tiled=True)
    partial_value = jnp.einsum("td,kdc->tkc", tokens, panels, preferred_element_type=jnp.float32)
    kv_out = lax.psum_scatter(partial_value, DP, scatter_dimension=2, tiled=True).astype(
        jnp.bfloat16
    )
    cotangent = lax.all_gather(d_kv, DP, axis=2, tiled=True)
    d_tokens = jnp.einsum(
        "tkc,kdc->td", cotangent, panels, preferred_element_type=jnp.float32
    ).astype(jnp.bfloat16)
    share = jnp.einsum("td,tkc->ckd", tokens, cotangent, preferred_element_type=jnp.float32)
    share = share.reshape(4, 8, 2, 16, 2, 1152)
    share = lax.psum_scatter(share, "z", scatter_dimension=1, tiled=True)
    share = lax.psum_scatter(share, "y", scatter_dimension=0, tiled=True)
    share = lax.psum_scatter(share, "xh", scatter_dimension=2, tiled=True)
    grad_kv = jnp.transpose(share.reshape(16, 2, 1152), (1, 2, 0))
    return (kv_out, d_tokens, grad_kv)


def solution(mesh):
    fine = Mesh(mesh.devices.reshape(2, 2, 4, 8, 2), DP + MP)
    return jax.shard_map(
        per_device,
        mesh=fine,
        in_specs=(P(MP, DP), P(None, DP, MP), P(MP, None, DP)),
        out_specs=(P(MP, None, DP), P(MP, DP), P(None, DP, MP)),
        check_vma=False,
    )
```

```python
import functools

import jax
import jax.numpy as jnp
from jax import lax
from jax.experimental import pallas as pl
from jax.experimental.pallas import tpu as pltpu
from jax.sharding import Mesh, PartitionSpec as P

MP = ("y", "z", "xh")
DP = ("xl", "core")
F32 = jnp.float32
BF16 = jnp.bfloat16
SMEM = pl.BlockSpec(memory_space=pltpu.SMEM)
COST = pl.CostEstimate(flops=1, bytes_accessed=1, transcendentals=0)
VMEM = pl.BlockSpec(memory_space=pltpu.VMEM)


def flip(x, axis, bits):
    n = lax.axis_size(axis)
    return lax.ppermute(x, axis, [(i, i ^ bits) for i in range(n)])


def put(x, piece, i):
    return lax.dynamic_update_index_in_dim(x, piece, i, 0)


def hold(*xs):
    return lax.optimization_barrier(xs)


def room(mib):
    return pltpu.CompilerParams(vmem_limit_bytes=mib * 2**20)


def shape(dims, dtype):
    return jax.ShapeDtypeStruct(dims, dtype)


def exponent(largest):
    return jnp.floor(jnp.log(jnp.maximum(largest, 1e-30)) * 1.4426950408889634)


def encode(x, e):
    u = x * jnp.exp2(13.0 - e)
    u2 = u * u
    return (u * jnp.abs(u) * u2 * (u2 * u2)).astype(BF16)


def decode(w, e):
    w = w.astype(F32)
    fourth = lax.rsqrt(lax.rsqrt(jnp.maximum(jnp.abs(w), 1e-37)))
    u = fourth * lax.rsqrt(fourth)
    return jnp.where(w > 0, u, jnp.where(w < 0, -u, 0.0)) * jnp.exp2(e - 13.0)


def largest_of(ref):
    return jnp.max(ref[...], axis=(0, 1), keepdims=True)


def grad_kernel(u_ref, p0, p1, p2, p3, tok, own, s1, s2, s3, acc, top):
    u = u_ref[0]
    top[...] = jnp.zeros_like(top)
    for r, p in enumerate((p0, p1, p2, p3)):
        g = lax.dot_general(p[...], tok[...], (((0,), (0,)), ((), ())), preferred_element_type=F32)
        acc[r ^ u] = g
        top[...] = jnp.maximum(top[...], jnp.max(jnp.abs(g).reshape(32, 8, 1152), axis=0))
    e = exponent(largest_of(top))
    own[...] = acc[0]
    for i, s in ((1, s1), (2, s2), (3, s3)):

        @pl.loop(0, 16)
        def _(j):
            rows = pl.ds(pl.multiple_of(j * 16, 16), 16)
            s[rows, :] = encode(acc[i, rows, :], e)

        s[256:272, :] = jnp.broadcast_to(e, (16, 1152)).astype(BF16)


def grad(u, pieces, tokens):
    return pl.pallas_call(
        grad_kernel,
        out_shape=[shape((256, 1152), F32)] + [shape((272, 1152), BF16)] * 3,
        in_specs=[SMEM] + [VMEM] * 5,
        out_specs=[VMEM] * 4,
        scratch_shapes=[pltpu.VMEM((4, 256, 1152), F32), pltpu.VMEM((8, 1152), F32)],
        compiler_params=room(16),
        cost_estimate=COST,
        name="grad",
    )(u, *pieces, tokens)


def sum_kernel(own, r1, r2, r3, out, acc, top):
    top[...] = jnp.zeros_like(top)
    es = [r[256:257, 0:1].astype(F32) for r in (r1, r2, r3)]

    @pl.loop(0, 16)
    def _(j):
        rows = pl.ds(pl.multiple_of(j * 16, 16), 16)
        x = own[rows, :]
        for r, e in zip((r1, r2, r3), es):
            x = x + decode(r[rows, :], e)
        acc[rows, :] = x
        top[...] = jnp.maximum(top[...], jnp.abs(x))

    e = exponent(largest_of(top))

    @pl.loop(0, 16)
    def _(j):
        rows = pl.ds(pl.multiple_of(j * 16, 16), 16)
        out[rows, :1152] = encode(acc[rows, :], e)
        out[rows, 1152:] = jnp.broadcast_to(e, (16, 128)).astype(BF16)


def sum_over_y(own, received):
    return pl.pallas_call(
        sum_kernel,
        out_shape=shape((256, 1280), BF16),
        in_specs=[VMEM] * 4,
        out_specs=VMEM,
        scratch_shapes=[pltpu.VMEM((256, 1152), F32), pltpu.VMEM((16, 1152), F32)],
        compiler_params=room(6),
        cost_estimate=COST,
        name="sum_over_y",
    )(own, *received)


def final_kernel(x, out):
    out[...] = jnp.zeros_like(out)

    @pl.loop(0, 16)
    def _(j):
        rows = pl.ds(pl.multiple_of(j * 16, 16), 16)
        out[...] += decode(x[rows, :1152], x[rows, 1152:1153].astype(F32))


def spread(x):
    return lax.all_to_all(x.reshape(16, 16, 1280), ("z", "xh"), 0, 0, tiled=True)


def sum_over_z(x):
    return pl.pallas_call(
        final_kernel,
        out_shape=shape((16, 1152), F32),
        in_specs=[VMEM],
        out_specs=VMEM,
        compiler_params=room(4),
        cost_estimate=COST,
        name="sum_over_z",
    )(x.reshape(256, 1280))


def encode12(x):
    e = exponent(jnp.max(jnp.abs(x), axis=(0, 1), keepdims=True))
    a = jnp.maximum(jnp.abs(x) * jnp.exp2(-e), 1e-30)
    w = jnp.exp2(12.0 * (jnp.log(a) * 1.4426950408889634) + 100.0)
    return jnp.where(x < 0, -w, w).astype(BF16), jnp.broadcast_to(e, (16, 256)).astype(BF16)


def decode12(w, e):
    w = w.astype(F32)
    a = jnp.maximum(jnp.abs(w), 1e-37)
    x = jnp.exp2((jnp.log(a) * 1.4426950408889634 - 100.0) * (1.0 / 12.0) + e)
    return jnp.where(w > 0, x, jnp.where(w < 0, -x, 0.0))


def project_kernel(quarters, adds, tok, w, *refs):
    n = len(quarters)
    added, outs = refs[: n * adds], refs[n * adds :]

    @pl.loop(0, 4)
    def _(j):
        rows = pl.ds(pl.multiple_of(j * 256, 256), 256)
        taller = pl.ds(pl.multiple_of(j * 272, 16), 272)
        for i, r in enumerate(quarters):
            x = lax.dot_general(
                tok[rows, :],
                w[:, r].reshape(256, 1152),
                (((1,), (1,)), ((), ())),
                preferred_element_type=F32,
            )
            for a in added[i * adds : (i + 1) * adds]:
                if a.shape[0] == 1088:
                    coded = a[taller, :]
                    x = x + decode12(coded[:256], coded[256:257, 0:1].astype(F32))
                else:
                    x = x + a[rows, :]
            if outs[i].shape[0] == 1088:
                outs[i][taller, :] = jnp.concatenate(encode12(x), axis=0)
            else:
                outs[i][rows, :] = x.astype(outs[i].dtype)


def project(tokens, w, quarters, added=(), dtype=F32, coded=False):
    n, adds = len(quarters), len(added) // len(quarters)
    return pl.pallas_call(
        functools.partial(project_kernel, quarters, adds),
        out_shape=[shape((1088 if coded else 1024, 256), dtype)] * n,
        in_specs=[VMEM] * (2 + len(added)),
        out_specs=[VMEM] * n,
        compiler_params=room(8),
        cost_estimate=COST,
        name="project",
    )(tokens, w, *added)


def back_kernel(p0, p1, p2, p3, w, *refs):
    out = refs[-1]
    flat = jnp.concatenate([w[:, r].reshape(256, 1152) for r in range(4)], axis=0)

    @pl.loop(0, 4)
    def _(j):
        rows = pl.ds(pl.multiple_of(j * 256, 256), 256)
        x = jnp.concatenate([p[rows, :] for p in (p0, p1, p2, p3)], axis=1)
        x = jnp.dot(x, flat, preferred_element_type=F32)
        for added in refs[:-1]:
            x = x + added[rows, :]
        out[rows, :] = x.astype(out.dtype)


def back(pieces, w, added=(), dtype=F32):
    return pl.pallas_call(
        back_kernel,
        out_shape=shape((1024, 1152), dtype),
        in_specs=[VMEM] * (5 + len(added)),
        out_specs=VMEM,
        compiler_params=room(12),
        cost_estimate=COST,
        name="back",
    )(*pieces, w, *added)


def per_device(tokens, kv_weight, d_kv):
    xl, core, y, xh = (lax.axis_index(a) for a in ("xl", "core", "y", "xh"))
    dp = 2 * xl + core
    u = (dp ^ y).reshape(1)

    own_k, own_v = d_kv[:, 0], d_kv[:, 1]
    wt = jnp.transpose(kv_weight, (0, 2, 1))

    both = put(put(jnp.zeros((2, *wt.shape), BF16), wt, xh), flip(wt, "xh", 1), xh ^ 1)
    both = jnp.transpose(both, (1, 0, 2, 3)).reshape(2, 32, 1152)
    beside_k, beside_v = flip(own_k, "core", 1), flip(own_v, "core", 1)
    both, own_k, own_v = hold(both, own_k, own_v)

    across_k = flip(own_k, "xl", 1)
    wy = put(jnp.zeros((4, 2, 32, 1152), BF16), both, y ^ dp)
    for bits in (1, 3, 2):
        wy = put(wy, flip(both, "y", bits), y ^ bits ^ dp)
    wk = lax.all_gather(wy[:, 0].reshape(128, 1152), "z", axis=0, tiled=True).reshape(8, 4, 32, 1152)
    wv = lax.all_gather(wy[:, 1].reshape(128, 1152), "z", axis=0, tiled=True).reshape(8, 4, 32, 1152)
    across_k, wy, own_v = hold(across_k, wy, own_v)

    across_v = flip(own_v, "xl", 1)
    corner_k = flip(across_k, "core", 1)
    gk, *send_k = grad(u, (own_k, beside_k, across_k, corner_k), tokens)
    got_k = [flip(s, "y", bits) for s, bits in zip(send_k, (1, 2, 3))]
    across_v, gk = hold(across_v, gk)
    corner_v = flip(across_v, "core", 1)
    gv, *send_v = grad(u, (own_v, beside_v, across_v, corner_v), tokens)
    got_v = [flip(s, "y", bits) for s, bits in zip(send_v, (1, 2, 3))]

    gv, gk, wk, *got_k = hold(gv, gk, wk, *got_k)
    to_far, to_near = project(tokens, wk, (3, 1))
    (far,) = project(tokens, wk, (2,), (flip(to_far, "core", 1),))
    near_k = flip(to_near, "core", 1)
    across = flip(far, "xl", 1)
    gk, far = hold(gk, far)
    total_k = spread(sum_over_y(gk, got_k))
    d_tokens = back((own_k, beside_k, across_k, corner_k), wk)
    total_k, across, d_tokens, gv, wv, near_k, *got_v = hold(
        total_k, across, d_tokens, gv, wv, near_k, *got_v
    )

    to_far, to_near = project(tokens, wv, (3, 1))
    (far,) = project(tokens, wv, (2,), (flip(to_far, "core", 1),), BF16, True)
    near_v = flip(to_near, "core", 1)
    across_out = flip(far, "xl", 1)
    gv, far, total_k, across = hold(gv, far, total_k, across)
    total_v = spread(sum_over_y(gv, got_v))
    grad_k = sum_over_z(total_k)
    (out_k,) = project(tokens, wk, (0,), (near_k, across), BF16)
    total_v, across_out, out_k, grad_k, wv = hold(total_v, across_out, out_k, grad_k, wv)
    grad_v = sum_over_z(total_v)
    (out_v,) = project(tokens, wv, (0,), (near_v, across_out), BF16)
    d_tokens = back((own_v, beside_v, across_v, corner_v), wv, (d_tokens,), BF16)
    kv_out = jnp.stack([out_k, out_v], axis=1)
    grad_kv = jnp.transpose(jnp.stack([grad_k, grad_v]), (0, 2, 1))
    return (kv_out, d_tokens, grad_kv)


def solution(mesh):
    fine = Mesh(mesh.devices.reshape(2, 2, 4, 8, 2), DP + MP)
    return jax.shard_map(
        per_device,
        mesh=fine,
        in_specs=(P(MP, DP), P(None, DP, MP), P(MP, None, DP)),
        out_specs=(P(MP, None, DP), P(MP, DP), P(None, DP, MP)),
        check_vma=False,
    )
```

```python
import functools

import jax
import jax.numpy as jnp
from jax import lax
from jax.experimental import pallas as pl
from jax.experimental.pallas import tpu as pltpu
from jax.sharding import Mesh, PartitionSpec as P

MP = ("y", "z", "xh")
DP = ("xl", "core")
F32 = jnp.float32
BF16 = jnp.bfloat16
SMEM = pl.BlockSpec(memory_space=pltpu.SMEM)
COST = pl.CostEstimate(flops=1, bytes_accessed=1, transcendentals=0)
VMEM = pl.BlockSpec(memory_space=pltpu.VMEM)


def flip(x, axis, bits):
    n = lax.axis_size(axis)
    return lax.ppermute(x, axis, [(i, i ^ bits) for i in range(n)])


def put(x, piece, i):
    return lax.dynamic_update_index_in_dim(x, piece, i, 0)


def hold(*xs):
    return lax.optimization_barrier(xs)


def room(mib):
    return pltpu.CompilerParams(vmem_limit_bytes=mib * 2**20)


def shape(dims, dtype):
    return jax.ShapeDtypeStruct(dims, dtype)


def exponent(largest):
    return jnp.floor(jnp.log(jnp.maximum(largest, 1e-30)) * 1.4426950408889634)


def encode(x, e):
    u = x * jnp.exp2(13.0 - e)
    u2 = u * u
    return (u * jnp.abs(u) * u2 * (u2 * u2)).astype(BF16)


def decode(w, e):
    w = w.astype(F32)
    fourth = lax.rsqrt(lax.rsqrt(jnp.maximum(jnp.abs(w), 1e-37)))
    u = fourth * lax.rsqrt(fourth)
    return jnp.where(w > 0, u, jnp.where(w < 0, -u, 0.0)) * jnp.exp2(e - 13.0)


def largest_of(ref):
    return jnp.max(ref[...], axis=(0, 1), keepdims=True)


def grad_kernel(u_ref, p0, p1, p2, p3, tok, own, s1, s2, s3, acc, top):
    u = u_ref[0]
    top[...] = jnp.zeros_like(top)
    for r, p in enumerate((p0, p1, p2, p3)):
        g = lax.dot_general(p[...], tok[...], (((0,), (0,)), ((), ())), preferred_element_type=F32)
        acc[r ^ u] = g
        top[...] = jnp.maximum(top[...], jnp.max(jnp.abs(g).reshape(32, 8, 1152), axis=0))
    e = exponent(largest_of(top))
    own[...] = acc[0]
    for i, s in ((1, s1), (2, s2), (3, s3)):

        @pl.loop(0, 16)
        def _(j):
            rows = pl.ds(pl.multiple_of(j * 16, 16), 16)
            s[rows, :] = encode(acc[i, rows, :], e)

        s[256:272, :] = jnp.broadcast_to(e, (16, 1152)).astype(BF16)


def grad(u, pieces, tokens):
    return pl.pallas_call(
        grad_kernel,
        out_shape=[shape((256, 1152), F32)] + [shape((272, 1152), BF16)] * 3,
        in_specs=[SMEM] + [VMEM] * 5,
        out_specs=[VMEM] * 4,
        scratch_shapes=[pltpu.VMEM((4, 256, 1152), F32), pltpu.VMEM((8, 1152), F32)],
        compiler_params=room(16),
        cost_estimate=COST,
        name="grad",
    )(u, *pieces, tokens)


def sum_kernel(*refs):
    groups, out, acc, top = (refs[:4], refs[4:8]), refs[8], refs[9], refs[10]
    for k, (own, *received) in enumerate(groups):
        top[...] = jnp.zeros_like(top)
        es = [r[256:257, 0:1].astype(F32) for r in received]

        @pl.loop(0, 16)
        def _(j):
            rows = pl.ds(pl.multiple_of(j * 16, 16), 16)
            x = own[rows, :]
            for r, e in zip(received, es):
                x = x + decode(r[rows, :], e)
            acc[rows, :] = x
            top[...] = jnp.maximum(top[...], jnp.abs(x))

        e = exponent(largest_of(top))

        @pl.loop(0, 16)
        def _(j):
            rows = pl.ds(pl.multiple_of(j * 16, 16), 16)
            to = pl.ds(pl.multiple_of(j * 32 + k * 16, 16), 16)
            out[to, :1152] = encode(acc[rows, :], e)
            out[to, 1152:] = jnp.broadcast_to(e, (16, 128)).astype(BF16)


def sum_over_y(*groups):
    return pl.pallas_call(
        sum_kernel,
        out_shape=shape((512, 1280), BF16),
        in_specs=[VMEM] * 8,
        out_specs=VMEM,
        scratch_shapes=[pltpu.VMEM((256, 1152), F32), pltpu.VMEM((16, 1152), F32)],
        compiler_params=room(6),
        cost_estimate=COST,
        name="sum_over_y",
    )(*groups)


def final_kernel(x, out):
    out[...] = jnp.zeros_like(out)

    @pl.loop(0, 16)
    def _(j):
        rows = pl.ds(pl.multiple_of(j * 32, 32), 32)
        out[...] += decode(x[rows, :1152], x[rows, 1152:1153].astype(F32))


def spread(x):
    return lax.all_to_all(x.reshape(16, 32, 1280), ("z", "xh"), 0, 0, tiled=True)


def sum_over_z(x):
    return pl.pallas_call(
        final_kernel,
        out_shape=shape((32, 1152), F32),
        in_specs=[VMEM],
        out_specs=VMEM,
        compiler_params=room(4),
        cost_estimate=COST,
        name="sum_over_z",
    )(x.reshape(512, 1280))


def encode12(x):
    e = exponent(jnp.max(jnp.abs(x), axis=(0, 1), keepdims=True))
    a = jnp.maximum(jnp.abs(x) * jnp.exp2(-e), 1e-30)
    w = jnp.exp2(12.0 * (jnp.log(a) * 1.4426950408889634) + 100.0)
    return jnp.where(x < 0, -w, w).astype(BF16), jnp.broadcast_to(e, (16, 256)).astype(BF16)


def decode12(w, e):
    w = w.astype(F32)
    a = jnp.maximum(jnp.abs(w), 1e-37)
    x = jnp.exp2((jnp.log(a) * 1.4426950408889634 - 100.0) * (1.0 / 12.0) + e)
    return jnp.where(w > 0, x, jnp.where(w < 0, -x, 0.0))


def product(tok, w, rows, r, k):
    columns = w[:, r, k].reshape(256, 1152)
    return lax.dot_general(
        tok[rows, :], columns, (((1,), (1,)), ((), ())), preferred_element_type=F32
    )


def each_block(body):
    for k in range(2):

        @pl.loop(0, 4)
        def _(j):
            i = j + 4 * k
            body(
                k,
                pl.ds(pl.multiple_of(j * 256, 256), 256),
                pl.ds(pl.multiple_of(i * 256, 256), 256),
                pl.ds(pl.multiple_of(i * 272, 16), 272),
            )


def beside_kernel(tok, w, to_far, to_near):
    def body(k, tokens, rows, coded):
        to_far[rows, :] = product(tok, w, tokens, 3, k)
        to_near[rows, :] = product(tok, w, tokens, 1, k)

    each_block(body)


def far_kernel(tok, w, got, out):
    def body(k, tokens, rows, coded):
        x = product(tok, w, tokens, 2, k) + got[rows, :]
        out[coded, :] = jnp.concatenate(encode12(x), axis=0)

    each_block(body)


def near_kernel(tok, w, got, across, out_k, out_v):
    def body(k, tokens, rows, coded):
        c = across[coded, :]
        x = product(tok, w, tokens, 0, k) + got[rows, :]
        x = x + decode12(c[:256], c[256:257, 0:1].astype(F32))
        (out_k, out_v)[k][tokens, :] = x.astype(BF16)

    each_block(body)


def project(kernel, outs, *args):
    return pl.pallas_call(
        kernel,
        out_shape=outs,
        in_specs=[VMEM] * len(args),
        out_specs=[VMEM] * len(outs),
        compiler_params=room(8),
        cost_estimate=COST,
        name=kernel.__name__,
    )(*args)


def back_kernel(*refs):
    pieces, w, out = refs[:8], refs[8], refs[9]
    flat = jnp.concatenate(
        [w[:, r, k].reshape(256, 1152) for k in range(2) for r in range(4)], axis=0
    )

    @pl.loop(0, 4)
    def _(j):
        rows = pl.ds(pl.multiple_of(j * 256, 256), 256)
        x = jnp.concatenate([p[rows, :] for p in pieces], axis=1)
        out[rows, :] = jnp.dot(x, flat, preferred_element_type=F32).astype(BF16)


def back(pieces, w):
    return pl.pallas_call(
        back_kernel,
        out_shape=shape((1024, 1152), BF16),
        in_specs=[VMEM] * 9,
        out_specs=VMEM,
        compiler_params=room(16),
        cost_estimate=COST,
        name="back",
    )(*pieces, w)


def per_device(tokens, kv_weight, d_kv):
    xl, core, y, xh = (lax.axis_index(a) for a in ("xl", "core", "y", "xh"))
    dp = 2 * xl + core
    u = (dp ^ y).reshape(1)

    own_k, own_v = d_kv[:, 0], d_kv[:, 1]
    wt = jnp.transpose(kv_weight, (0, 2, 1))

    both = put(put(jnp.zeros((2, *wt.shape), BF16), wt, xh), flip(wt, "xh", 1), xh ^ 1)
    both = jnp.transpose(both, (1, 0, 2, 3)).reshape(2, 32, 1152)
    beside_k, beside_v = flip(own_k, "core", 1), flip(own_v, "core", 1)
    both, own_k, own_v = hold(both, own_k, own_v)

    first = flip(own_k[:512], "xl", 1)
    got_w = [flip(both, "y", bits) for bits in (1, 2, 3)]
    first, second, both, *got_w = hold(first, own_k[512:], both, *got_w)
    second = flip(second, "xl", 1)
    w = put(jnp.zeros((4, 2, 32, 1152), BF16), both, y ^ dp)
    for bits, piece in zip((1, 2, 3), got_w):
        w = put(w, piece, y ^ bits ^ dp)
    w = lax.all_gather(w.reshape(256, 1152), "z", axis=0, tiled=True).reshape(8, 4, 2, 32, 1152)
    second, own_v = hold(second, own_v)

    across_v = flip(own_v, "xl", 1)
    across_k = jnp.concatenate([first, second])
    corner_k = flip(across_k, "core", 1)
    gk, *send_k = grad(u, (own_k, beside_k, across_k, corner_k), tokens)
    got_k = [flip(s, "y", bits) for s, bits in zip(send_k, (1, 2, 3))]
    across_v, gk = hold(across_v, gk)
    corner_v = flip(across_v, "core", 1)
    gv, *send_v = grad(u, (own_v, beside_v, across_v, corner_v), tokens)
    got_v = [flip(s, "y", bits) for s, bits in zip(send_v, (1, 2, 3))]
    gk, gv, w, got_v[1], *got_k = hold(gk, gv, w, got_v[1], *got_k)

    both_cores = shape((2048, 256), F32)
    to_far, to_near = project(beside_kernel, [both_cores] * 2, tokens, w)
    got_far, got_near = flip(to_far, "core", 1), flip(to_near, "core", 1)
    got_far, got_near, gk, gv, *got = hold(got_far, got_near, gk, gv, *got_k, *got_v)
    total = spread(sum_over_y(gk, *got[:3], gv, *got[3:]))
    (far,) = project(far_kernel, [shape((2176, 256), BF16)], tokens, w, got_far)
    across = flip(far, "xl", 1)
    d_tokens = back(
        (own_k, beside_k, across_k, corner_k, own_v, beside_v, across_v, corner_v), w
    )
    total, across, d_tokens, got_near = hold(total, across, d_tokens, got_near)
    out_k, out_v = project(
        near_kernel, [shape((1024, 256), BF16)] * 2, tokens, w, got_near, across
    )
    grads = sum_over_z(total).reshape(2, 16, 1152)
    kv_out = jnp.stack([out_k, out_v], axis=1)
    grad_kv = jnp.transpose(grads, (0, 2, 1))
    return (kv_out, d_tokens, grad_kv)


def solution(mesh):
    fine = Mesh(mesh.devices.reshape(2, 2, 4, 8, 2), DP + MP)
    return jax.shard_map(
        per_device,
        mesh=fine,
        in_specs=(P(MP, DP), P(None, DP, MP), P(MP, None, DP)),
        out_specs=(P(MP, None, DP), P(MP, DP), P(None, DP, MP)),
        check_vma=False,
    )
```

```python
import functools

import jax
import jax.numpy as jnp
from jax import lax
from jax.experimental import pallas as pl
from jax.experimental.pallas import tpu as pltpu
from jax.sharding import Mesh, PartitionSpec as P

MP = ("y", "z", "xh")
DP = ("xl", "core")
F32 = jnp.float32
BF16 = jnp.bfloat16
SMEM = pl.BlockSpec(memory_space=pltpu.SMEM)
COST = pl.CostEstimate(flops=1, bytes_accessed=1, transcendentals=0)
VMEM = pl.BlockSpec(memory_space=pltpu.VMEM)


def flip(x, axis, bits):
    n = lax.axis_size(axis)
    return lax.ppermute(x, axis, [(i, i ^ bits) for i in range(n)])


def put(x, piece, i):
    return lax.dynamic_update_index_in_dim(x, piece, i, 0)


def hold(*xs):
    return lax.optimization_barrier(xs)


def room(mib):
    return pltpu.CompilerParams(vmem_limit_bytes=mib * 2**20)


def shape(dims, dtype):
    return jax.ShapeDtypeStruct(dims, dtype)


def exponent(largest):
    return jnp.floor(jnp.log(jnp.maximum(largest, 1e-30)) * 1.4426950408889634)


def encode(x, e):
    u = x * jnp.exp2(13.0 - e)
    u2 = u * u
    return (u * jnp.abs(u) * u2 * (u2 * u2)).astype(BF16)


def decode(w, e):
    w = w.astype(F32)
    fourth = lax.rsqrt(lax.rsqrt(jnp.maximum(jnp.abs(w), 1e-37)))
    u = fourth * lax.rsqrt(fourth)
    return jnp.where(w > 0, u, jnp.where(w < 0, -u, 0.0)) * jnp.exp2(e - 13.0)


def largest_of(ref):
    return jnp.max(ref[...], axis=(0, 1), keepdims=True)


def grad_kernel(u_ref, p0, p1, p2, p3, tok, own, s1, s2, s3, acc, top):
    u = u_ref[0]
    top[...] = jnp.zeros_like(top)
    for r, p in enumerate((p0, p1, p2, p3)):
        g = lax.dot_general(p[...], tok[...], (((0,), (0,)), ((), ())), preferred_element_type=F32)
        acc[r ^ u] = g
        top[...] = jnp.maximum(top[...], jnp.max(jnp.abs(g).reshape(32, 8, 1152), axis=0))
    e = exponent(largest_of(top))
    own[...] = acc[0]
    for i, s in ((1, s1), (2, s2), (3, s3)):

        @pl.loop(0, 16)
        def _(j):
            rows = pl.ds(pl.multiple_of(j * 16, 16), 16)
            s[rows, :] = encode(acc[i, rows, :], e)

        s[256:272, :] = jnp.broadcast_to(e, (16, 1152)).astype(BF16)


def grad(u, pieces, tokens):
    return pl.pallas_call(
        grad_kernel,
        out_shape=[shape((256, 1152), F32)] + [shape((272, 1152), BF16)] * 3,
        in_specs=[SMEM] + [VMEM] * 5,
        out_specs=[VMEM] * 4,
        scratch_shapes=[pltpu.VMEM((4, 256, 1152), F32), pltpu.VMEM((8, 1152), F32)],
        compiler_params=room(16),
        cost_estimate=COST,
        name="grad",
    )(u, *pieces, tokens)


def sum_kernel(*refs):
    groups, out, acc, top = (refs[:4], refs[4:8]), refs[8], refs[9], refs[10]
    for k, (own, *received) in enumerate(groups):
        top[...] = jnp.zeros_like(top)
        es = [r[256:257, 0:1].astype(F32) for r in received]

        @pl.loop(0, 16)
        def _(j):
            rows = pl.ds(pl.multiple_of(j * 16, 16), 16)
            x = own[rows, :]
            for r, e in zip(received, es):
                x = x + decode(r[rows, :], e)
            acc[rows, :] = x
            top[...] = jnp.maximum(top[...], jnp.abs(x))

        e = exponent(largest_of(top))

        @pl.loop(0, 16)
        def _(j):
            rows = pl.ds(pl.multiple_of(j * 16, 16), 16)
            to = pl.ds(pl.multiple_of(j * 32 + k * 16, 16), 16)
            out[to, :1152] = encode(acc[rows, :], e)
            out[to, 1152:] = jnp.broadcast_to(e, (16, 128)).astype(BF16)


def sum_over_y(*groups):
    return pl.pallas_call(
        sum_kernel,
        out_shape=shape((512, 1280), BF16),
        in_specs=[VMEM] * 8,
        out_specs=VMEM,
        scratch_shapes=[pltpu.VMEM((256, 1152), F32), pltpu.VMEM((16, 1152), F32)],
        compiler_params=room(6),
        cost_estimate=COST,
        name="sum_over_y",
    )(*groups)


def final_kernel(x, out):
    out[...] = jnp.zeros_like(out)

    @pl.loop(0, 16)
    def _(j):
        rows = pl.ds(pl.multiple_of(j * 32, 32), 32)
        out[...] += decode(x[rows, :1152], x[rows, 1152:1153].astype(F32))


def spread(x):
    return lax.all_to_all(x.reshape(16, 32, 1280), ("z", "xh"), 0, 0, tiled=True)


def sum_over_z(x):
    return pl.pallas_call(
        final_kernel,
        out_shape=shape((32, 1152), F32),
        in_specs=[VMEM],
        out_specs=VMEM,
        compiler_params=room(4),
        cost_estimate=COST,
        name="sum_over_z",
    )(x.reshape(512, 1280))


def encode12(x):
    e = exponent(jnp.max(jnp.abs(x), axis=(0, 1), keepdims=True))
    a = jnp.maximum(jnp.abs(x) * jnp.exp2(-e), 1e-30)
    w = jnp.exp2(12.0 * (jnp.log(a) * 1.4426950408889634) + 100.0)
    return jnp.where(x < 0, -w, w).astype(BF16), jnp.broadcast_to(e, (16, 256)).astype(BF16)


def decode12(w, e):
    w = w.astype(F32)
    a = jnp.maximum(jnp.abs(w), 1e-37)
    x = jnp.exp2((jnp.log(a) * 1.4426950408889634 - 100.0) * (1.0 / 12.0) + e)
    return jnp.where(w > 0, x, jnp.where(w < 0, -x, 0.0))


def product(tok, w, rows, r, k):
    columns = w[:, r, k].reshape(256, 1152)
    return lax.dot_general(
        tok[rows, :], columns, (((1,), (1,)), ((), ())), preferred_element_type=F32
    )


def each_block(body):
    for k in range(2):

        @pl.loop(0, 4)
        def _(j):
            i = j + 4 * k
            body(
                k,
                pl.ds(pl.multiple_of(j * 256, 256), 256),
                pl.ds(pl.multiple_of(i * 256, 256), 256),
                pl.ds(pl.multiple_of(i * 272, 16), 272),
            )


def beside_kernel(tok, w, to_far, to_near):
    def body(k, tokens, rows, coded):
        to_far[rows, :] = product(tok, w, tokens, 3, k)
        to_near[rows, :] = product(tok, w, tokens, 1, k)

    each_block(body)


def far_kernel(tok, w, got, out):
    def body(k, tokens, rows, coded):
        x = product(tok, w, tokens, 2, k) + got[rows, :]
        out[coded, :] = jnp.concatenate(encode12(x), axis=0)

    each_block(body)


def near_kernel(tok, w, got, across, out_k, out_v):
    def body(k, tokens, rows, coded):
        c = across[coded, :]
        x = product(tok, w, tokens, 0, k) + got[rows, :]
        x = x + decode12(c[:256], c[256:257, 0:1].astype(F32))
        (out_k, out_v)[k][tokens, :] = x.astype(BF16)

    each_block(body)


def project(kernel, outs, *args):
    return pl.pallas_call(
        kernel,
        out_shape=outs,
        in_specs=[VMEM] * len(args),
        out_specs=[VMEM] * len(outs),
        compiler_params=room(8),
        cost_estimate=COST,
        name=kernel.__name__,
    )(*args)


def back_kernel(*refs):
    pieces, w, out = refs[:8], refs[8], refs[9]
    flat = jnp.concatenate(
        [w[:, r, k].reshape(256, 1152) for k in range(2) for r in range(4)], axis=0
    )

    @pl.loop(0, 4)
    def _(j):
        rows = pl.ds(pl.multiple_of(j * 256, 256), 256)
        x = jnp.concatenate([p[rows, :] for p in pieces], axis=1)
        out[rows, :] = jnp.dot(x, flat, preferred_element_type=F32).astype(BF16)


def back(pieces, w):
    return pl.pallas_call(
        back_kernel,
        out_shape=shape((1024, 1152), BF16),
        in_specs=[VMEM] * 9,
        out_specs=VMEM,
        compiler_params=room(16),
        cost_estimate=COST,
        name="back",
    )(*pieces, w)


def per_device(tokens, kv_weight, d_kv):
    xl, core, y, xh = (lax.axis_index(a) for a in ("xl", "core", "y", "xh"))
    dp = 2 * xl + core
    u = (dp ^ y).reshape(1)

    own_k, own_v = d_kv[:, 0], d_kv[:, 1]
    wt = jnp.transpose(kv_weight, (0, 2, 1))

    both = put(put(jnp.zeros((2, *wt.shape), BF16), wt, xh), flip(wt, "xh", 1), xh ^ 1)
    both = jnp.transpose(both, (1, 0, 2, 3)).reshape(2, 32, 1152)
    beside_k, beside_v = flip(own_k, "core", 1), flip(own_v, "core", 1)
    both, own_k, own_v = hold(both, own_k, own_v)

    first = flip(own_k[:512], "xl", 1)
    got_w = [flip(both, "y", bits) for bits in (1, 2, 3)]
    first, second, both, *got_w = hold(first, own_k[512:], both, *got_w)
    second = flip(second, "xl", 1)
    w = put(jnp.zeros((4, 2, 32, 1152), BF16), both, y ^ dp)
    for bits, piece in zip((1, 2, 3), got_w):
        w = put(w, piece, y ^ bits ^ dp)
    w = lax.all_gather(w.reshape(256, 1152), "z", axis=0, tiled=True).reshape(8, 4, 2, 32, 1152)
    second, own_v = hold(second, own_v)

    across_v = flip(own_v, "xl", 1)
    across_k = jnp.concatenate([first, second])
    corner_k = flip(across_k, "core", 1)
    gk, *send_k = grad(u, (own_k, beside_k, across_k, corner_k), tokens)
    got_k = [flip(s, "y", bits) for s, bits in zip(send_k, (1, 2, 3))]
    across_v, gk = hold(across_v, gk)
    corner_v = flip(across_v, "core", 1)
    gv, *send_v = grad(u, (own_v, beside_v, across_v, corner_v), tokens)
    got_v = [flip(s, "y", bits) for s, bits in zip(send_v, (1, 2, 3))]
    gk, gv, w, *got = hold(gk, gv, w, *got_k, *got_v)

    both_cores = shape((2048, 256), F32)
    to_far, to_near = project(beside_kernel, [both_cores] * 2, tokens, w)
    got_far, got_near = flip(to_far, "core", 1), flip(to_near, "core", 1)
    total = sum_over_y(gk, *got[:3], gv, *got[3:])
    (far,) = project(far_kernel, [shape((2176, 256), BF16)], tokens, w, got_far)
    total, far, got_near, w = hold(total, far, got_near, w)
    across = flip(far, "xl", 1)
    total = spread(total)
    d_tokens = back(
        (own_k, beside_k, across_k, corner_k, own_v, beside_v, across_v, corner_v), w
    )
    total, across, d_tokens, got_near = hold(total, across, d_tokens, got_near)
    out_k, out_v = project(
        near_kernel, [shape((1024, 256), BF16)] * 2, tokens, w, got_near, across
    )
    grads = sum_over_z(total).reshape(2, 16, 1152)
    kv_out = jnp.stack([out_k, out_v], axis=1)
    grad_kv = jnp.transpose(grads, (0, 2, 1))
    return (kv_out, d_tokens, grad_kv)


def solution(mesh):
    fine = Mesh(mesh.devices.reshape(2, 2, 4, 8, 2), DP + MP)
    return jax.shard_map(
        per_device,
        mesh=fine,
        in_specs=(P(MP, DP), P(None, DP, MP), P(MP, None, DP)),
        out_specs=(P(MP, None, DP), P(MP, DP), P(None, DP, MP)),
        check_vma=False,
    )
```

```python
import functools

import jax
import jax.numpy as jnp
from jax import lax
from jax.experimental import pallas as pl
from jax.experimental.pallas import tpu as pltpu
from jax.sharding import Mesh, PartitionSpec as P

MP = ("y", "z", "xh")
DP = ("xl", "core")
F32 = jnp.float32
BF16 = jnp.bfloat16
SMEM = pl.BlockSpec(memory_space=pltpu.SMEM)
COST = pl.CostEstimate(flops=1, bytes_accessed=1, transcendentals=0)
VMEM = pl.BlockSpec(memory_space=pltpu.VMEM)


def flip(x, axis, bits):
    n = lax.axis_size(axis)
    return lax.ppermute(x, axis, [(i, i ^ bits) for i in range(n)])


def put(x, piece, i):
    return lax.dynamic_update_index_in_dim(x, piece, i, 0)


def hold(*xs):
    return lax.optimization_barrier(xs)


def room(mib):
    return pltpu.CompilerParams(vmem_limit_bytes=mib * 2**20)


def shape(dims, dtype):
    return jax.ShapeDtypeStruct(dims, dtype)


def exponent(largest):
    return jnp.floor(jnp.log(jnp.maximum(largest, 1e-30)) * 1.4426950408889634)


def encode(x, e):
    u = x * jnp.exp2(13.0 - e)
    u2 = u * u
    return (u * jnp.abs(u) * u2 * (u2 * u2)).astype(BF16)


def decode(w, e):
    w = w.astype(F32)
    fourth = lax.rsqrt(lax.rsqrt(jnp.maximum(jnp.abs(w), 1e-37)))
    u = fourth * lax.rsqrt(fourth)
    return jnp.where(w > 0, u, jnp.where(w < 0, -u, 0.0)) * jnp.exp2(e - 13.0)


def largest_of(ref):
    return jnp.max(ref[...], axis=(0, 1), keepdims=True)


def grad_kernel(u_ref, p0, p1, p2, p3, tok, own, s1, s2, s3, acc, top):
    u = u_ref[0]
    top[...] = jnp.zeros_like(top)
    for r, p in enumerate((p0, p1, p2, p3)):
        g = lax.dot_general(p[...], tok[...], (((0,), (0,)), ((), ())), preferred_element_type=F32)
        acc[r ^ u] = g
        top[...] = jnp.maximum(top[...], jnp.max(jnp.abs(g).reshape(32, 8, 1152), axis=0))
    e = exponent(largest_of(top))
    own[...] = acc[0]
    for i, s in ((1, s1), (2, s2), (3, s3)):

        @pl.loop(0, 16)
        def _(j):
            rows = pl.ds(pl.multiple_of(j * 16, 16), 16)
            s[rows, :] = encode(acc[i, rows, :], e)

        s[256:272, :] = jnp.broadcast_to(e, (16, 1152)).astype(BF16)


def grad(u, pieces, tokens):
    return pl.pallas_call(
        grad_kernel,
        out_shape=[shape((256, 1152), F32)] + [shape((272, 1152), BF16)] * 3,
        in_specs=[SMEM] + [VMEM] * 5,
        out_specs=[VMEM] * 4,
        scratch_shapes=[pltpu.VMEM((4, 256, 1152), F32), pltpu.VMEM((8, 1152), F32)],
        compiler_params=room(16),
        cost_estimate=COST,
        name="grad",
    )(u, *pieces, tokens)


def sum_kernel(*refs):
    groups, out, acc, top = (refs[:4], refs[4:8]), refs[8], refs[9], refs[10]
    for k, (own, *received) in enumerate(groups):
        top[...] = jnp.zeros_like(top)
        es = [r[256:257, 0:1].astype(F32) for r in received]

        @pl.loop(0, 16)
        def _(j):
            rows = pl.ds(pl.multiple_of(j * 16, 16), 16)
            x = own[rows, :]
            for r, e in zip(received, es):
                x = x + decode(r[rows, :], e)
            acc[rows, :] = x
            top[...] = jnp.maximum(top[...], jnp.abs(x))

        e = exponent(largest_of(top))

        @pl.loop(0, 16)
        def _(j):
            rows = pl.ds(pl.multiple_of(j * 16, 16), 16)
            to = pl.ds(pl.multiple_of(j * 32 + k * 16, 16), 16)
            out[to, :1152] = encode(acc[rows, :], e)
            out[to, 1152:] = jnp.broadcast_to(e, (16, 128)).astype(BF16)


def sum_over_y(*groups):
    return pl.pallas_call(
        sum_kernel,
        out_shape=shape((512, 1280), BF16),
        in_specs=[VMEM] * 8,
        out_specs=VMEM,
        scratch_shapes=[pltpu.VMEM((256, 1152), F32), pltpu.VMEM((16, 1152), F32)],
        compiler_params=room(6),
        cost_estimate=COST,
        name="sum_over_y",
    )(*groups)


def final_kernel(x, out):
    out[...] = jnp.zeros_like(out)

    @pl.loop(0, 16)
    def _(j):
        rows = pl.ds(pl.multiple_of(j * 32, 32), 32)
        out[...] += decode(x[rows, :1152], x[rows, 1152:1153].astype(F32))


def spread(x):
    return lax.all_to_all(x.reshape(16, 32, 1280), ("z", "xh"), 0, 0, tiled=True)


def sum_over_z(x):
    return pl.pallas_call(
        final_kernel,
        out_shape=shape((32, 1152), F32),
        in_specs=[VMEM],
        out_specs=VMEM,
        compiler_params=room(4),
        cost_estimate=COST,
        name="sum_over_z",
    )(x.reshape(512, 1280))


def encode12(x):
    e = exponent(jnp.max(jnp.abs(x), axis=(0, 1), keepdims=True))
    a = jnp.maximum(jnp.abs(x) * jnp.exp2(-e), 1e-30)
    w = jnp.exp2(12.0 * (jnp.log(a) * 1.4426950408889634) + 100.0)
    return jnp.where(x < 0, -w, w).astype(BF16), jnp.broadcast_to(e, (16, 256)).astype(BF16)


def decode12(w, e):
    w = w.astype(F32)
    a = jnp.maximum(jnp.abs(w), 1e-37)
    x = jnp.exp2((jnp.log(a) * 1.4426950408889634 - 100.0) * (1.0 / 12.0) + e)
    return jnp.where(w > 0, x, jnp.where(w < 0, -x, 0.0))


def product(tok, w, rows, r, k):
    columns = w[:, r, k].reshape(256, 1152)
    return lax.dot_general(
        tok[rows, :], columns, (((1,), (1,)), ((), ())), preferred_element_type=F32
    )


def each_block(body):
    for k in range(2):

        @pl.loop(0, 4)
        def _(j):
            i = j + 4 * k
            body(
                k,
                pl.ds(pl.multiple_of(j * 256, 256), 256),
                pl.ds(pl.multiple_of(i * 256, 256), 256),
                pl.ds(pl.multiple_of(i * 272, 16), 272),
            )


def beside_kernel(tok, w, to_far, to_near):
    def body(k, tokens, rows, coded):
        to_far[rows, :] = product(tok, w, tokens, 3, k)
        to_near[rows, :] = product(tok, w, tokens, 1, k)

    each_block(body)


def far_kernel(tok, w, got, out):
    def body(k, tokens, rows, coded):
        x = product(tok, w, tokens, 2, k) + got[rows, :]
        out[coded, :] = jnp.concatenate(encode12(x), axis=0)

    each_block(body)


def near_kernel(tok, w, got, across, out_k, out_v):
    def body(k, tokens, rows, coded):
        c = across[coded, :]
        x = product(tok, w, tokens, 0, k) + got[rows, :]
        x = x + decode12(c[:256], c[256:257, 0:1].astype(F32))
        (out_k, out_v)[k][tokens, :] = x.astype(BF16)

    each_block(body)


def project(kernel, outs, *args):
    return pl.pallas_call(
        kernel,
        out_shape=outs,
        in_specs=[VMEM] * len(args),
        out_specs=[VMEM] * len(outs),
        compiler_params=room(8),
        cost_estimate=COST,
        name=kernel.__name__,
    )(*args)


def back_kernel(*refs):
    pieces, w, out = refs[:8], refs[8], refs[9]
    flat = jnp.concatenate(
        [w[:, r, k].reshape(256, 1152) for k in range(2) for r in range(4)], axis=0
    )

    @pl.loop(0, 4)
    def _(j):
        rows = pl.ds(pl.multiple_of(j * 256, 256), 256)
        x = jnp.concatenate([p[rows, :] for p in pieces], axis=1)
        out[rows, :] = jnp.dot(x, flat, preferred_element_type=F32).astype(BF16)


def back(pieces, w):
    return pl.pallas_call(
        back_kernel,
        out_shape=shape((1024, 1152), BF16),
        in_specs=[VMEM] * 9,
        out_specs=VMEM,
        compiler_params=room(16),
        cost_estimate=COST,
        name="back",
    )(*pieces, w)


def per_device(tokens, kv_weight, d_kv):
    xl, core, y, xh = (lax.axis_index(a) for a in ("xl", "core", "y", "xh"))
    dp = 2 * xl + core
    u = (dp ^ y).reshape(1)

    own_k, own_v = d_kv[:, 0], d_kv[:, 1]
    wt = jnp.transpose(kv_weight, (0, 2, 1))

    both = put(put(jnp.zeros((2, *wt.shape), BF16), wt, xh), flip(wt, "xh", 1), xh ^ 1)
    both = jnp.transpose(both, (1, 0, 2, 3)).reshape(2, 32, 1152)
    beside_k, beside_v = flip(own_k, "core", 1), flip(own_v, "core", 1)
    both, own_k, own_v = hold(both, own_k, own_v)

    first = flip(own_k[:512], "xl", 1)
    got_w = [flip(both, "y", bits) for bits in (1, 2, 3)]
    first, second, both, *got_w = hold(first, own_k[512:], both, *got_w)
    second = flip(second, "xl", 1)
    w = put(jnp.zeros((4, 2, 32, 1152), BF16), both, y ^ dp)
    for bits, piece in zip((1, 2, 3), got_w):
        w = put(w, piece, y ^ bits ^ dp)
    w = lax.all_gather(w.reshape(256, 1152), "z", axis=0, tiled=True).reshape(8, 4, 2, 32, 1152)
    second, own_v = hold(second, own_v)

    across_v = flip(own_v, "xl", 1)
    across_k = jnp.concatenate([first, second])
    corner_k = flip(across_k, "core", 1)
    gk, *send_k = grad(u, (own_k, beside_k, across_k, corner_k), tokens)
    got_k = [flip(s, "y", bits) for s, bits in zip(send_k, (1, 2, 3))]
    across_v, gk = hold(across_v, gk)
    corner_v = flip(across_v, "core", 1)
    gv, *send_v = grad(u, (own_v, beside_v, across_v, corner_v), tokens)
    got_v = [flip(s, "y", bits) for s, bits in zip(send_v, (1, 2, 3))]
    gk, gv, w, got_v[0], *got_k = hold(gk, gv, w, got_v[0], *got_k)

    both_cores = shape((2048, 256), F32)
    to_far, to_near = project(beside_kernel, [both_cores] * 2, tokens, w)
    got_far, got_near = flip(to_far, "core", 1), flip(to_near, "core", 1)
    (far,) = project(far_kernel, [shape((2176, 256), BF16)], tokens, w, got_far)
    across = flip(far, "xl", 1)
    total = sum_over_y(gk, *got_k, gv, *got_v)
    d_tokens = back(
        (own_k, beside_k, across_k, corner_k, own_v, beside_v, across_v, corner_v), w
    )
    total, across, d_tokens, got_near = hold(total, across, d_tokens, got_near)
    total = spread(total)
    out_k, out_v = project(
        near_kernel, [shape((1024, 256), BF16)] * 2, tokens, w, got_near, across
    )
    grads = sum_over_z(total).reshape(2, 16, 1152)
    kv_out = jnp.stack([out_k, out_v], axis=1)
    grad_kv = jnp.transpose(grads, (0, 2, 1))
    return (kv_out, d_tokens, grad_kv)


def solution(mesh):
    fine = Mesh(mesh.devices.reshape(2, 2, 4, 8, 2), DP + MP)
    return jax.shard_map(
        per_device,
        mesh=fine,
        in_specs=(P(MP, DP), P(None, DP, MP), P(MP, None, DP)),
        out_specs=(P(MP, None, DP), P(MP, DP), P(None, DP, MP)),
        check_vma=False,
    )
```
